128 devices in a mesh: dp: 2 (over x_lo), tok: 64 (over y, x_hi, z, core).
Axes of the slice: x: 4 (x_hi: 2, x_lo: 2; x = x_hi * 2 + x_lo), y: 4, z: 4, core: 2. Of those that a mesh axis runs over, the one named last changes fastest.
Arguments:
- row_input: bfloat16 [64, 1024, 1024], P('tok', None, 'dp'), may hold values from -6 to 6
- out_grad: bfloat16 [64, 1024, 1024], P('tok', None, 'dp'), may hold values from -6 to 6
- in_weight: bfloat16 [2, 64, 1024, 1024], P(None, 'tok'), may hold values from -0.1875 to 0.1875
- out_weight: bfloat16 [2, 64, 1024, 1024], P(None, 'tok'), may hold values from -0.1875 to 0.1875
Outputs:
- grad_rows: bfloat16 [64, 1024, 1024], P('tok', None, 'dp')
- grad_in_weight: bfloat16 [2, 64, 1024, 1024], P(None, 'tok', 'dp')
- grad_out_weight: bfloat16 [2, 64, 1024, 1024], P(None, 'tok', None, 'dp')
The draws below stay inside these ranges and needn't reach their ends.
All inputs are finite; a program needn't handle non-finite values.
Results may differ from the reference program's by a relative error of at most 0.015.
Values may be sent and summed in bfloat16 or wider, within the bound.
No kernel may reach another device: no remote copies, remote signals or barrier semaphores. Data moves between devices by JAX's collectives and lax.ppermute only.
A program may use at most 128 MiB of HBM per device.

```python
import jax
import jax.numpy as jnp
from jax import lax

D = 1024
H = 1024
T_SIZE = 64
ROWS_DEV = 512
ROWS = 1024
BLOCKS = 2
N_DP = 2


def block_levels(key, dims, pieces, low, high):
    loudness = 1.0
    for dim, blocks in pieces:
        steps = jax.random.uniform(jax.random.fold_in(jax.random.fold_in(key, 6), dim), (blocks,), jnp.float32, low / len(pieces), high / len(pieces))
        loudness = loudness * jnp.repeat(jnp.exp(steps), dims[dim] // blocks).reshape((-1,) + (1,) * (len(dims) - 1 - dim))
    return loudness


def bell_draw(key, shape, width, limit, shards=(), held_as=jnp.bfloat16):
    gain = block_levels(key, shape, shards, -0.22, 0.18) if shards else 1.0
    result = jax.random.normal(key, shape, jnp.float32) * width * gain
    return jnp.minimum(jnp.maximum(result, -limit), limit).astype(held_as)


def setup_inputs(seed: int = 0) -> dict:
    seeds = jax.random.split(jax.random.key(seed), 5)
    return {
        "row_input": bell_draw(seeds[0], (T_SIZE, D, ROWS), 1.0, 6.0, ((0, 64), (2, 2))),
        "out_grad": bell_draw(seeds[1], (T_SIZE, D, ROWS), 1.0, 6.0, ((0, 64), (2, 2))),
        "in_weight": bell_draw(seeds[2], (BLOCKS, T_SIZE, D, H), D ** -0.5, 0.1875, ((1, 64),)),
        "out_weight": bell_draw(seeds[3], (BLOCKS, T_SIZE, H, D), H ** -0.5, 0.1875, ((1, 64),)),
    }


epsilon = 1e-05

def mixing(values):
    token_count, feature_width, row_count = values.shape
    head_size = feature_width // token_count
    grouped = values.reshape(token_count, token_count, head_size, row_count)
    return grouped.transpose(1, 0, 2, 3).reshape(token_count, feature_width, row_count)

def normalize(values):
    center = values - lax.optimization_barrier(jnp.mean(values, axis=1, keepdims=True))
    inverse = lax.rsqrt(lax.optimization_barrier(jnp.mean(center * center, axis=1, keepdims=True)) + epsilon)
    return (center * inverse, inverse)

def norm_back(normal, inverse, upward):
    mean_up = lax.optimization_barrier(jnp.mean(upward, axis=1, keepdims=True))
    mean_cross = lax.optimization_barrier(jnp.mean(upward * normal, axis=1, keepdims=True))
    return inverse * (upward - mean_up - normal * mean_cross)

def gelu_parts(hidden):
    cumulative = 0.5 * (1.0 + lax.erf(hidden * 0.7071067811865476))
    density = jnp.exp(-0.5 * hidden * hidden) * 0.3989422804014327
    return (hidden * cumulative, cumulative + hidden * density)

def row_block_sum(left_side, right_side, form):
    total_sum = None
    for number in range(N_DP):
        offset = number * ROWS_DEV
        left_rows = left_side[:, :, offset:offset + ROWS_DEV].astype(jnp.float32)
        right_rows = right_side[:, :, offset:offset + ROWS_DEV].astype(jnp.float32)
        term_sum = jnp.einsum(form, left_rows, right_rows)
        rounded = lax.optimization_barrier(term_sum.astype(jnp.bfloat16)).astype(jnp.float32)
        total_sum = rounded if total_sum is None else total_sum + rounded
    return total_sum.astype(jnp.bfloat16)

def reference(row_input, out_grad, in_weight, out_weight):
    caches = []
    current = row_input
    for number in range(BLOCKS):
        weight_first = in_weight[number].astype(jnp.float32)
        weight_second = out_weight[number].astype(jnp.float32)
        mixture = mixing(current)
        summed = mixture.astype(jnp.float32) + current.astype(jnp.float32)
        summed_hat, summed_inv = normalize(summed)
        normed = summed_hat.astype(jnp.bfloat16)
        hidden = jnp.einsum('tdh,tdr->thr', weight_first, normed.astype(jnp.float32))
        active_full, derivative = gelu_parts(hidden)
        active = active_full.astype(jnp.bfloat16)
        second = jnp.einsum('thd,thr->tdr', weight_second, active.astype(jnp.float32)) + normed.astype(jnp.float32)
        second_hat, second_inv = normalize(second)
        caches.append((summed_hat, summed_inv, normed, derivative, active, second_hat, second_inv))
        current = second_hat.astype(jnp.bfloat16)
    upward = out_grad
    grads_first = [None] * BLOCKS
    grads_second = [None] * BLOCKS
    for number in reversed(range(BLOCKS)):
        summed_hat, summed_inv, normed, derivative, active, second_hat, second_inv = caches[number]
        weight_first = in_weight[number].astype(jnp.float32)
        weight_second = out_weight[number].astype(jnp.float32)
        dsecond = norm_back(second_hat, second_inv, upward.astype(jnp.float32))
        dsecond_low = dsecond.astype(jnp.bfloat16)
        dhidden = (jnp.einsum('thd,tdr->thr', weight_second, dsecond_low.astype(jnp.float32)) * derivative).astype(jnp.bfloat16)
        inner = jnp.einsum('tdh,thr->tdr', weight_first, dhidden.astype(jnp.float32)) + dsecond
        dsummed = norm_back(summed_hat, summed_inv, inner)
        dsummed_low = dsummed.astype(jnp.bfloat16)
        upward = (dsummed + mixing(dsummed_low).astype(jnp.float32)).astype(jnp.bfloat16)
        grads_second[number] = row_block_sum(active, dsecond_low, 'thr,tdr->thd')
        grads_first[number] = row_block_sum(normed, dhidden, 'tdr,thr->tdh')
    return (upward, jnp.stack(grads_first), jnp.stack(grads_second))
```

```python
import collections
import functools

import jax
import jax.numpy as jnp
from jax import lax
from jax.experimental import pallas as pl
from jax.experimental.pallas import tpu as pltpu
from jax.sharding import PartitionSpec as P

epsilon = 1e-05
BF = jnp.bfloat16
F32 = jnp.float32
BOTH = ("dp", "tok")
GRANT = 60 << 20
STEP = 32
CHUNK = 256


def permute(value, pairs):
    tokens = lax.axis_size("tok")
    table = [
        (dp * tokens + base + last, to_dp * tokens + base + to_last)
        for base in range(0, tokens, 2)
        for (dp, last), (to_dp, to_last) in pairs
    ]
    return lax.ppermute(value, BOTH, table)


ACROSS = (((0, 1), (1, 0)), ((1, 0), (0, 1)))
STAY = (((0, 0), (0, 0)), ((1, 1), (1, 1)))
BESIDE = (((0, 0), (0, 1)), ((0, 1), (0, 0)), ((1, 0), (1, 1)), ((1, 1), (1, 0)))
HAND = (((0, 0), (0, 1)), ((1, 1), (1, 0)))


def swap(value):
    return permute(value, ACROSS)


def other_core(value):
    return permute(value, BESIDE)


def mix(value):
    tokens = lax.axis_size("tok")
    depth, rows = value.shape
    parts = value.reshape(tokens, depth // tokens, rows)
    groups = [
        [dp * tokens + base + last for base in range(0, tokens, 2) for dp in range(2)] for last in range(2)
    ]
    arrived = lax.all_to_all(
        parts, BOTH, split_axis=0, concat_axis=0, axis_index_groups=groups, tiled=True
    )
    return arrived.reshape(depth, rows)


def nn(left, right):
    return lax.dot_general(left, right, (((1,), (0,)), ((), ())), preferred_element_type=F32)


def nt(left, right):
    return lax.dot_general(left, right, (((1,), (1,)), ((), ())), preferred_element_type=F32)


def gelu_parts(hidden):
    cumulative = 0.5 * (1.0 + lax.erf(hidden * 0.7071067811865476))
    density = jnp.exp(-0.5 * hidden * hidden) * 0.3989422804014327
    return hidden * cumulative, cumulative + hidden * density


def fold(value):
    depth, rows = value.shape
    return jnp.sum(value.reshape(depth // 8, 8, rows), axis=0)


def total(value):
    return jnp.sum(value, axis=0, keepdims=True)


def pieces(start, stop, size):
    return [pl.ds(at, size) for at in range(start, stop, size)]


Moves = collections.namedtuple("Moves", ("start", "fetch", "emit", "post_half", "finish"))


def copies(sems):
    used, pending = [], []

    def start(source, target):
        copy = pltpu.make_async_copy(source, target, sems.at[len(used)])
        used.append(copy)
        copy.start()
        return copy

    def fetch(source, target, size=CHUNK):
        return [start(source.at[part, :], target.at[part, :]) for part in pieces(0, target.shape[0], size)]

    def emit(source, target, part):
        pending.append(start(source.at[part, :], target.at[part, :]))

    def post_half(source, target, place):
        half = target.shape[0]
        other = pl.ds(pl.multiple_of((1 - place[0]) * half, half), half)
        pending.append(start(source.at[other, :], target))

    def finish():
        for copy in pending:
            copy.wait()

    return Moves(start, fetch, emit, post_half, finish)


def norm_stats(values, depth, first):
    mean = total(first) * (1.0 / depth)
    second = jnp.zeros_like(first)
    for part in pieces(0, depth, STEP):
        center = values[part, :] - mean
        second += fold(center * center)
    return mean, lax.rsqrt(total(second) * (1.0 / depth) + epsilon)


def forward_part(inputs, w_in_t, w_out_t, waits, normed, active, derivative, summed, second, done):
    depth, rows = summed.shape
    mixed, current, mixed_waits, current_waits = inputs
    acc = jnp.zeros((8, rows), F32)
    for number, big in enumerate(range(0, depth, CHUNK)):
        mixed_waits[number].wait()
        current_waits[number].wait()
        for part in pieces(big, big + CHUNK, STEP):
            value = mixed[part, :].astype(F32) + current[part, :].astype(F32)
            summed[part, :] = value
            acc += fold(value)
    mean, inverse_s = norm_stats(summed, depth, acc)
    for big in range(0, depth, CHUNK):
        for part in pieces(big, big + CHUNK, STEP):
            normed[part, :] = ((summed[part, :] - mean) * inverse_s).astype(BF)
        done("normed", pl.ds(big, CHUNK))
    for number, big in enumerate(range(0, w_in_t.shape[0], CHUNK)):
        waits[0][number].wait()
        hidden = nn(w_in_t[pl.ds(big, CHUNK), :], normed[...])
        for small in range(0, CHUNK, STEP):
            act, der = gelu_parts(hidden[small : small + STEP])
            active[pl.ds(big + small, STEP), :] = act.astype(BF)
            derivative[pl.ds(big + small, STEP), :] = der.astype(derivative.dtype)
        done("active", pl.ds(big, CHUNK))
    acc = jnp.zeros((8, rows), F32)
    for number, big in enumerate(range(0, depth, CHUNK)):
        waits[1][number].wait()
        part = pl.ds(big, CHUNK)
        value = nn(w_out_t[part, :], active[...]) + normed[part, :].astype(F32)
        second[part, :] = value
        acc += fold(value)
    mean, inverse_2 = norm_stats(second, depth, acc)
    return inverse_s, mean, inverse_2


def forward_kernel(number, place, mixed, current, w_in_t, w_out_t, normed, active, derivative, following, inverse_s,
                   inverse_2, normed_send, b_mixed, b_current, b_in, b_out, b_normed, b_active, b_derivative, b_following,
                   b_inverse_s, b_inverse_2, summed, second, sems):
    moves = copies(sems)
    inputs = (b_mixed, b_current, moves.fetch(mixed, b_mixed), moves.fetch(current, b_current))
    waits = (moves.fetch(w_in_t.at[number], b_in), moves.fetch(w_out_t.at[number], b_out))
    depth, rows = summed.shape

    def done(name, part):
        if name == "normed":
            moves.emit(b_normed, normed, part)
        else:
            moves.emit(b_active, active, part)
            moves.emit(b_derivative, derivative, part)
        if name == "active" and part.start == 0:
            moves.post_half(b_normed, normed_send, place)

    inv_s, mean, inv_2 = forward_part(
        inputs, b_in, b_out, waits, b_normed, b_active, b_derivative, summed, second, done
    )
    b_inverse_s[...] = jnp.broadcast_to(inv_s, (8, rows))
    b_inverse_2[...] = jnp.broadcast_to(inv_2, (8, rows))
    moves.emit(b_inverse_s, inverse_s, pl.ds(0, 8))
    moves.emit(b_inverse_2, inverse_2, pl.ds(0, 8))
    for big in range(0, depth, CHUNK):
        for part in pieces(big, big + CHUNK, STEP):
            b_following[part, :] = ((second[part, :] - mean) * inv_2).astype(BF)
        moves.emit(b_following, following, pl.ds(big, CHUNK))
    moves.finish()


def backward_part(read_hat, read_up, inverse_2, inverse_s, w_out, w_in, waits, normed, derivative,
                  dsecond_low, dhidden, dsummed, dsecond, done):
    depth, rows = normed.shape
    up_acc = jnp.zeros((8, rows), F32)
    cross_acc = jnp.zeros((8, rows), F32)
    for part in pieces(0, depth, STEP):
        upward = read_up(part)
        up_acc += fold(upward)
        cross_acc += fold(upward * read_hat(part))
    mean_up = total(up_acc) * (1.0 / depth)
    mean_cross = total(cross_acc) * (1.0 / depth)
    for big in range(0, depth, CHUNK):
        for part in pieces(big, big + CHUNK, STEP):
            value = inverse_2 * (read_up(part) - mean_up - read_hat(part) * mean_cross)
            dsecond[part, :] = value
            dsecond_low[part, :] = value.astype(BF)
        done("dsecond_low", pl.ds(big, CHUNK))
    for number, big in enumerate(range(0, w_out.shape[0], CHUNK)):
        waits[0][number].wait()
        part = pl.ds(big, CHUNK)
        value = nn(w_out[part, :], dsecond_low[...])
        dhidden[part, :] = (value * derivative[part, :].astype(F32)).astype(BF)
        done("dhidden", part)
    up_acc = jnp.zeros((8, rows), F32)
    cross_acc = jnp.zeros((8, rows), F32)
    for number, big in enumerate(range(0, depth, CHUNK)):
        waits[1][number].wait()
        part = pl.ds(big, CHUNK)
        value = nn(w_in[part, :], dhidden[...]) + dsecond[part, :]
        dsecond[part, :] = value
        up_acc += fold(value)
        cross_acc += fold(value * normed[part, :].astype(F32))
    mean_up = total(up_acc) * (1.0 / depth)
    mean_cross = total(cross_acc) * (1.0 / depth)
    for big in range(0, depth, CHUNK):
        for part in pieces(big, big + CHUNK, STEP):
            value = inverse_s * (dsecond[part, :] - mean_up - normed[part, :].astype(F32) * mean_cross)
            dsummed[part, :] = value.astype(BF)
        done("dsummed", pl.ds(big, CHUNK))


def turn_kernel(number, place, moved, mixed, current, grad_own, grad_got, w_in_t, w_out_t, w_in, w_out,
                normed, active, dsecond_low, dhidden, dsummed, normed_send, dsecond_send,
                b_mixed, b_current, b_grad, holds, b_normed, b_active, b_dsecond_low, b_dhidden, b_dsummed,
                derivative, summed, second, dsecond, sems, grad_sem):
    moves = copies(sems)
    inputs = (b_mixed, b_current, moves.fetch(mixed, b_mixed), moves.fetch(current, b_current))
    waits = [
        moves.fetch(ref.at[number], holds.at[at]) for at, ref in enumerate((w_in_t, w_out_t, w_out, w_in))
    ]

    @pl.when(moved[0] == 1)
    def _():
        pltpu.make_async_copy(grad_got, b_grad, grad_sem.at[0]).start()

    @pl.when(moved[0] == 0)
    def _():
        pltpu.make_async_copy(grad_own, b_grad, grad_sem.at[0]).start()

    depth, rows = summed.shape
    pairs = {
        "normed": (b_normed, normed),
        "active": (b_active, active),
        "dsecond_low": (b_dsecond_low, dsecond_low),
        "dhidden": (b_dhidden, dhidden),
        "dsummed": (b_dsummed, dsummed),
    }

    def done(name, part):
        moves.emit(*pairs[name], part)
        if name == "active" and part.start == 0:
            moves.post_half(b_normed, normed_send, place)
        if name == "dhidden" and part.start == 0:
            moves.post_half(b_dsecond_low, dsecond_send, place)

    inv_s, mean, inv_2 = forward_part(
        inputs, holds.at[0], holds.at[1], waits[:2], b_normed, b_active, derivative, summed, second, done
    )
    for part in pieces(0, depth, STEP):
        second[part, :] = (second[part, :] - mean) * inv_2
    pltpu.make_async_copy(grad_own, b_grad, grad_sem.at[0]).wait()
    backward_part(
        lambda part: second[part, :], lambda part: b_grad[part, :].astype(F32), inv_2, inv_s,
        holds.at[2], holds.at[3], waits[2:], b_normed, derivative, b_dsecond_low, b_dhidden, b_dsummed, dsecond, done,
    )
    moves.finish()


def backward_kernel(number, place, carried, returned, following, normed, derivative, inverse_s, inverse_2, w_in, w_out,
                    dsecond_low, dhidden, dsummed, dsecond_send,
                    b_carried, b_returned, b_following, b_normed, b_derivative, b_inverse_s, b_inverse_2, holds,
                    b_dsecond_low, b_dhidden, b_dsummed, dsecond, sems):
    moves = copies(sems)
    first = (
        moves.fetch(carried, b_carried) + moves.fetch(returned, b_returned) + moves.fetch(following, b_following)
        + moves.fetch(inverse_s, b_inverse_s, 8) + moves.fetch(inverse_2, b_inverse_2, 8)
    )
    waits = [moves.fetch(w_out.at[number], holds.at[0])]
    early = moves.fetch(derivative, b_derivative) + moves.fetch(normed, b_normed)
    waits.append(moves.fetch(w_in.at[number], holds.at[1]))
    pairs = {
        "dsecond_low": (b_dsecond_low, dsecond_low),
        "dhidden": (b_dhidden, dhidden),
        "dsummed": (b_dsummed, dsummed),
    }

    def done(name, part):
        moves.emit(*pairs[name], part)
        if name == "dhidden" and part.start == 0:
            moves.post_half(b_dsecond_low, dsecond_send, place)

    def read_up(part):
        value = b_carried[part, :].astype(F32) + b_returned[part, :].astype(F32)
        return value.astype(BF).astype(F32)

    for copy in first + early:
        copy.wait()
    backward_part(
        lambda part: b_following[part, :].astype(F32), read_up, b_inverse_2[0:1, :], b_inverse_s[0:1, :],
        holds.at[0], holds.at[1], waits, b_normed, b_derivative, b_dsecond_low, b_dhidden, b_dsummed, dsecond, done,
    )
    moves.finish()


def grads_kernel(place, normed, dhidden, active, dsecond_low, normed_got, dhidden_got, active_got, dsecond_got,
                 sum_in, sum_out, b_normed, b_dhidden, b_active, b_dsecond_low, b_in, b_out, sems):
    moves = copies(sems)
    half = normed_got.shape[0]
    own = pl.ds(pl.multiple_of(place[0] * half, half), half)
    first = [moves.start(normed.at[own, :], b_normed.at[0]), moves.start(dhidden, b_dhidden.at[0])]
    first += [moves.start(normed_got, b_normed.at[1]), moves.start(dhidden_got, b_dhidden.at[1])]
    then = [moves.start(dsecond_low.at[own, :], b_dsecond_low.at[0]), moves.start(active, b_active.at[0])]
    then += [moves.start(dsecond_got, b_dsecond_low.at[1]), moves.start(active_got, b_active.at[1])]
    for copy in first:
        copy.wait()
    for part in pieces(0, half, CHUNK):
        term = nt(b_normed[0, part, :], b_dhidden[0]) + nt(b_normed[1, part, :], b_dhidden[1])
        b_in[part, :] = term.astype(BF)
        moves.emit(b_in, sum_in, part)
    for copy in then:
        copy.wait()
    for part in pieces(0, active.shape[0], CHUNK):
        term = nt(b_active[0, part, :], b_dsecond_low[0]) + nt(b_active[1, part, :], b_dsecond_low[1])
        b_out[part, :] = term.astype(BF)
        moves.emit(b_out, sum_out, part)
    moves.finish()


def weights_kernel(place, in_own, in_got, out_own, out_got, w_in, w_out, w_in_t, w_out_t):
    @pl.when(place[0] == 1)
    def _():
        w_in[...] = in_got[...]
        w_out[...] = out_got[...]

    @pl.when(place[0] == 0)
    def _():
        w_in[...] = in_own[...]
        w_out[...] = out_own[...]

    w_in_t[0] = w_in[0].T
    w_out_t[0] = w_out[0].T


def launch(kernel, outs, scratch, work, scalars, *operands):
    return pl.pallas_call(
        kernel,
        out_shape=[jax.ShapeDtypeStruct(shape, dtype) for shape, dtype in outs],
        in_specs=[SMEM] * scalars + [ANY] * (len(operands) - scalars),
        out_specs=[ANY] * len(outs),
        scratch_shapes=[pltpu.VMEM(*item) if isinstance(item, tuple) else pltpu.SemaphoreType.DMA((item,))
                        for item in scratch],
        compiler_params=pltpu.CompilerParams(vmem_limit_bytes=GRANT),
        cost_estimate=pl.CostEstimate(flops=0, bytes_accessed=work << 20, transcendentals=0),
    )(*operands)


SMEM = pl.BlockSpec(memory_space=pltpu.SMEM)
ANY = pl.BlockSpec(memory_space=pl.ANY)


def pick_weights(moved, in_own, in_got, out_own, out_got):
    blocks, depth, width = in_own.shape
    spec = pl.BlockSpec((1, depth, width), lambda k: (k, 0, 0))
    out = jax.ShapeDtypeStruct(in_own.shape, BF)
    return pl.pallas_call(
        weights_kernel,
        grid=(blocks,),
        out_shape=[out] * 4,
        in_specs=[SMEM] + [spec] * 4,
        out_specs=[spec] * 4,
        compiler_params=pltpu.CompilerParams(vmem_limit_bytes=GRANT),
        cost_estimate=pl.CostEstimate(flops=0, bytes_accessed=32 << 20, transcendentals=0),
    )(moved, in_own, in_got, out_own, out_got)


def grads(core, normed, dhidden, active, dsecond_low, *got):
    depth, rows = normed.shape
    width = active.shape[0]
    half = depth // 2
    outs = [((half, width), BF), ((width, half), BF)]
    scratch = [((2, half, rows), BF), ((2, width, rows), BF), ((2, width, rows), BF), ((2, half, rows), BF), *outs, 40]
    return launch(grads_kernel, outs, scratch, 10, 1, core, normed, dhidden, active, dsecond_low, *got)


def run_forward(number, core, mixed, current, w_in_t, w_out_t):
    tall = mixed.shape
    depth, rows = tall
    width = w_in_t.shape[1]
    wide, line = (width, rows), (8, rows)
    outs = [(tall, BF), (wide, BF), (wide, BF), (tall, BF), (line, F32), (line, F32)]
    half = ((depth // 2, rows), BF)
    scratch = [(tall, BF), (tall, BF), ((width, depth), BF), ((depth, width), BF), *outs, (tall, F32), (tall, F32), 60]
    return launch(functools.partial(forward_kernel, number), outs + [half], scratch, 16, 1,
                core, mixed, current, w_in_t, w_out_t)


def run_turn(number, core, moved, mixed, current, grad_own, grad_got, w_in_t, w_out_t, w_in, w_out):
    tall = mixed.shape
    depth, rows = tall
    width = w_in_t.shape[1]
    wide = (width, rows)
    outs = [(tall, BF), (wide, BF), (tall, BF), (wide, BF), (tall, BF)]
    scratch = [(tall, BF)] * 3 + [((4, depth, width), BF), *outs, (wide, F32), (tall, F32), (tall, F32), (tall, F32),
                                  80, 1]
    return launch(functools.partial(turn_kernel, number), outs + [((depth // 2, rows), BF)] * 2, scratch, 24, 2,
                core, moved, mixed, current, grad_own, grad_got, w_in_t, w_out_t, w_in, w_out)


def run_backward(number, core, carried, returned, following, normed, derivative, inverse_s, inverse_2, w_in, w_out):
    tall = carried.shape
    depth, rows = tall
    width = w_in.shape[2]
    wide, line = (width, rows), (8, rows)
    outs = [(tall, BF), (wide, BF), (tall, BF)]
    scratch = [(tall, BF), (tall, BF), (tall, BF), (tall, BF), (wide, BF), (line, F32), (line, F32),
               ((2, width, depth), BF), *outs, (tall, F32), 60]
    return launch(functools.partial(backward_kernel, number), outs + [((depth // 2, rows), BF)], scratch, 16, 1,
                core, carried, returned, following, normed, derivative, inverse_s, inverse_2, w_in, w_out)


def per_device(row_input, out_grad, in_weight, out_weight):
    row_input, out_grad = row_input[0], out_grad[0]
    in_weight, out_weight = in_weight[:, 0], out_weight[:, 0]
    last = lax.axis_index("tok") % 2
    core = last.astype(jnp.int32).reshape(1)
    is_moved = last != lax.axis_index("dp")
    moved = is_moved.astype(jnp.int32).reshape(1)

    def chosen(got, own):
        return jnp.where(is_moved, got, own)

    current = permute(row_input, ACROSS + STAY)
    got_in = permute(in_weight, HAND)
    got_out = permute(out_weight, HAND)
    current, got_in, got_out, out_grad = lax.optimization_barrier((current, got_in, got_out, out_grad))
    mixed = mix(current)
    w_in, w_out, w_in_t, w_out_t = pick_weights(moved, in_weight, got_in, out_weight, got_out)
    grad_got = swap(out_grad)
    normed_0, active_0, derivative_0, following_0, inverse_s_0, inverse_2_0, normed_send_0 = run_forward(
        0, core, mixed, current, w_in_t, w_out_t
    )
    mixed = mix(following_0)
    normed_got_0, active_got_0 = other_core(normed_send_0), other_core(active_0)
    normed_1, active_1, dsecond_low_1, dhidden_1, dsummed_1, normed_send_1, dsecond_send_1 = run_turn(
        1, core, moved, mixed, following_0, out_grad, grad_got, w_in_t, w_out_t, w_in, w_out
    )
    returned = mix(dsummed_1)
    sums_1 = grads(core, normed_1, dhidden_1, active_1, dsecond_low_1,
                   *[other_core(value) for value in (normed_send_1, dhidden_1, active_1, dsecond_send_1)])
    swapped_1 = [swap(value) for value in sums_1]
    returned, _ = lax.optimization_barrier((returned, sums_1))
    dsecond_low_0, dhidden_0, dsummed_0, dsecond_send_0 = run_backward(
        0, core, dsummed_1, returned, following_0, normed_0, derivative_0, inverse_s_0, inverse_2_0, w_in, w_out
    )
    dsummed_0, swapped_1[0] = lax.optimization_barrier((dsummed_0, swapped_1[0]))
    returned = mix(dsummed_0)
    dsecond_low_0, swapped_1[1] = lax.optimization_barrier((dsecond_low_0, swapped_1[1]))
    sums_0 = grads(core, normed_0, dhidden_0, active_0, dsecond_low_0,
                   normed_got_0, other_core(dhidden_0), active_got_0, other_core(dsecond_send_0))
    swapped_0 = [swap(value) for value in sums_0]
    grad_rows = (dsummed_0.astype(F32) + returned.astype(F32)).astype(BF)
    grad_rows = chosen(swap(grad_rows), grad_rows)
    grad_in = chosen(jnp.stack([swapped_0[0], swapped_1[0]]), jnp.stack([sums_0[0], sums_1[0]]))
    grad_out = chosen(jnp.stack([swapped_0[1], swapped_1[1]]), jnp.stack([sums_0[1], sums_1[1]]))
    return grad_rows[None], grad_in[:, None], grad_out[:, None]


def solution(mesh):
    return jax.shard_map(
        per_device,
        mesh=mesh,
        in_specs=(
            P("tok", None, "dp"),
            P("tok", None, "dp"),
            P(None, "tok", None, None),
            P(None, "tok", None, None),
        ),
        out_specs=(P("tok", None, "dp"), P(None, "tok", "dp", None), P(None, "tok", None, "dp")),
        check_vma=False,
    )
```

```python
import collections
import functools

import jax
import jax.numpy as jnp
from jax import lax
from jax.experimental import pallas as pl
from jax.experimental.pallas import tpu as pltpu
from jax.sharding import PartitionSpec as P

epsilon = 1e-05
BF = jnp.bfloat16
F32 = jnp.float32
BOTH = ("dp", "tok")
GRANT = 63 << 20
STEP = 32
CHUNK = 512


def permute(value, pairs):
    tokens = lax.axis_size("tok")
    table = [
        (dp * tokens + base + last, to_dp * tokens + base + to_last)
        for base in range(0, tokens, 2)
        for (dp, last), (to_dp, to_last) in pairs
    ]
    return lax.ppermute(value, BOTH, table)


ACROSS = (((0, 1), (1, 0)), ((1, 0), (0, 1)))
STAY = (((0, 0), (0, 0)), ((1, 1), (1, 1)))
BESIDE = (((0, 0), (0, 1)), ((0, 1), (0, 0)), ((1, 0), (1, 1)), ((1, 1), (1, 0)))
HAND = (((0, 0), (0, 1)), ((1, 1), (1, 0)))


def swap(value):
    return permute(value, ACROSS)


def other_core(value):
    return permute(value, BESIDE)


def mix(value):
    tokens = lax.axis_size("tok")
    depth, rows = value.shape
    parts = value.reshape(tokens, depth // tokens, rows)
    groups = [
        [dp * tokens + base + last for base in range(0, tokens, 2) for dp in range(2)] for last in range(2)
    ]
    arrived = lax.all_to_all(
        parts, BOTH, split_axis=0, concat_axis=0, axis_index_groups=groups, tiled=True
    )
    return arrived.reshape(depth, rows)


def nn(left, right):
    return lax.dot_general(left, right, (((1,), (0,)), ((), ())), preferred_element_type=F32)


def nt(left, right):
    return lax.dot_general(left, right, (((1,), (1,)), ((), ())), preferred_element_type=F32)


def gelu_parts(hidden):
    cumulative = 0.5 * (1.0 + lax.erf(hidden * 0.7071067811865476))
    density = jnp.exp(-0.5 * hidden * hidden) * 0.3989422804014327
    return hidden * cumulative, cumulative + hidden * density


def fold(value):
    depth, rows = value.shape
    return jnp.sum(value.reshape(depth // 8, 8, rows), axis=0)


def total(value):
    return jnp.sum(value, axis=0, keepdims=True)


def pieces(start, stop, size):
    return [pl.ds(at, size) for at in range(start, stop, size)]


Moves = collections.namedtuple("Moves", ("start", "fetch", "emit", "post_half", "finish"))


def copies(sems):
    used, pending = [], []

    def start(source, target):
        copy = pltpu.make_async_copy(source, target, sems.at[len(used)])
        used.append(copy)
        copy.start()
        return copy

    def fetch(source, target, size=CHUNK):
        return [start(source.at[part, :], target.at[part, :]) for part in pieces(0, target.shape[0], size)]

    def emit(source, target, part):
        pending.append(start(source.at[part, :], target.at[part, :]))

    def post_half(source, target, place):
        half = target.shape[0]
        other = pl.ds(pl.multiple_of((1 - place[0]) * half, half), half)
        pending.append(start(source.at[other, :], target))

    def finish():
        for copy in pending:
            copy.wait()

    return Moves(start, fetch, emit, post_half, finish)


def norm_stats(values, depth, first):
    mean = total(first) * (1.0 / depth)
    second = jnp.zeros_like(first)
    for part in pieces(0, depth, STEP):
        center = values[part, :] - mean
        second += fold(center * center)
    return mean, lax.rsqrt(total(second) * (1.0 / depth) + epsilon)


def forward_part(inputs, w_in_t, w_out_t, waits, normed, active, derivative, summed, second, done):
    depth, rows = summed.shape
    mixed, current, mixed_waits, current_waits = inputs
    acc = jnp.zeros((8, rows), F32)
    for number, big in enumerate(range(0, depth, CHUNK)):
        mixed_waits[number].wait()
        current_waits[number].wait()
        for part in pieces(big, big + CHUNK, STEP):
            value = mixed[part, :].astype(F32) + current[part, :].astype(F32)
            summed[part, :] = value
            acc += fold(value)
    mean, inverse_s = norm_stats(summed, depth, acc)
    for big in range(0, depth, CHUNK):
        for part in pieces(big, big + CHUNK, STEP):
            normed[part, :] = ((summed[part, :] - mean) * inverse_s).astype(BF)
        done("normed", pl.ds(big, CHUNK))
    for number, big in enumerate(range(0, w_in_t.shape[0], CHUNK)):
        waits[0][number].wait()
        hidden = nn(w_in_t[pl.ds(big, CHUNK), :], normed[...])
        for small in range(0, CHUNK, STEP):
            act, der = gelu_parts(hidden[small : small + STEP])
            active[pl.ds(big + small, STEP), :] = act.astype(BF)
            derivative[pl.ds(big + small, STEP), :] = der.astype(derivative.dtype)
        done("active", pl.ds(big, CHUNK))
    acc = jnp.zeros((8, rows), F32)
    for number, big in enumerate(range(0, depth, CHUNK)):
        waits[1][number].wait()
        part = pl.ds(big, CHUNK)
        value = nn(w_out_t[part, :], active[...]) + normed[part, :].astype(F32)
        second[part, :] = value
        acc += fold(value)
    mean, inverse_2 = norm_stats(second, depth, acc)
    return inverse_s, mean, inverse_2


def forward_kernel(number, place, mixed, current, w_in_t, w_out_t, normed, active, derivative, following, inverse_s,
                   inverse_2, normed_send, b_mixed, b_current, b_in, b_out, b_normed, b_active, b_derivative, b_following,
                   b_inverse_s, b_inverse_2, summed, second, sems):
    moves = copies(sems)
    inputs = (b_mixed, b_current, moves.fetch(mixed, b_mixed), moves.fetch(current, b_current))
    waits = (moves.fetch(w_in_t.at[number], b_in), moves.fetch(w_out_t.at[number], b_out))
    depth, rows = summed.shape

    def done(name, part):
        if name == "normed":
            moves.emit(b_normed, normed, part)
        else:
            moves.emit(b_active, active, part)
            moves.emit(b_derivative, derivative, part)
        if name == "active" and part.start == 0:
            moves.post_half(b_normed, normed_send, place)

    inv_s, mean, inv_2 = forward_part(
        inputs, b_in, b_out, waits, b_normed, b_active, b_derivative, summed, second, done
    )
    b_inverse_s[...] = jnp.broadcast_to(inv_s, (8, rows))
    b_inverse_2[...] = jnp.broadcast_to(inv_2, (8, rows))
    moves.emit(b_inverse_s, inverse_s, pl.ds(0, 8))
    moves.emit(b_inverse_2, inverse_2, pl.ds(0, 8))
    for big in range(0, depth, CHUNK):
        for part in pieces(big, big + CHUNK, STEP):
            b_following[part, :] = ((second[part, :] - mean) * inv_2).astype(BF)
        moves.emit(b_following, following, pl.ds(big, CHUNK))
    moves.finish()


def backward_part(read_hat, read_up, inverse_2, inverse_s, w_out, w_in, waits, normed, derivative,
                  dsecond_low, dhidden, dsummed, dsecond, done):
    depth, rows = normed.shape
    up_acc = jnp.zeros((8, rows), F32)
    cross_acc = jnp.zeros((8, rows), F32)
    for part in pieces(0, depth, STEP):
        upward = read_up(part)
        up_acc += fold(upward)
        cross_acc += fold(upward * read_hat(part))
    mean_up = total(up_acc) * (1.0 / depth)
    mean_cross = total(cross_acc) * (1.0 / depth)
    for big in range(0, depth, CHUNK):
        for part in pieces(big, big + CHUNK, STEP):
            value = inverse_2 * (read_up(part) - mean_up - read_hat(part) * mean_cross)
            dsecond[part, :] = value
            dsecond_low[part, :] = value.astype(BF)
        done("dsecond_low", pl.ds(big, CHUNK))
    for number, big in enumerate(range(0, w_out.shape[0], CHUNK)):
        waits[0][number].wait()
        part = pl.ds(big, CHUNK)
        value = nn(w_out[part, :], dsecond_low[...])
        dhidden[part, :] = (value * derivative[part, :].astype(F32)).astype(BF)
        done("dhidden", part)
    up_acc = jnp.zeros((8, rows), F32)
    cross_acc = jnp.zeros((8, rows), F32)
    for number, big in enumerate(range(0, depth, CHUNK)):
        waits[1][number].wait()
        part = pl.ds(big, CHUNK)
        value = nn(w_in[part, :], dhidden[...]) + dsecond[part, :]
        dsecond[part, :] = value
        up_acc += fold(value)
        cross_acc += fold(value * normed[part, :].astype(F32))
    mean_up = total(up_acc) * (1.0 / depth)
    mean_cross = total(cross_acc) * (1.0 / depth)
    for big in range(0, depth, CHUNK):
        for part in pieces(big, big + CHUNK, STEP):
            value = inverse_s * (dsecond[part, :] - mean_up - normed[part, :].astype(F32) * mean_cross)
            dsummed[part, :] = value.astype(BF)
        done("dsummed", pl.ds(big, CHUNK))


def turn_kernel(number, place, moved, mixed, current, grad_own, grad_got, w_in_t, w_out_t, w_in, w_out,
                normed, active, dsecond_low, dhidden, dsummed, normed_send, dsecond_send,
                b_mixed, b_current, b_grad, holds, b_normed, b_active, b_dsecond_low, b_dhidden, b_dsummed,
                derivative, summed, second, dsecond, sems, grad_sem):
    moves = copies(sems)
    inputs = (b_mixed, b_current, moves.fetch(mixed, b_mixed), moves.fetch(current, b_current))
    waits = [
        moves.fetch(ref.at[number], holds.at[at]) for at, ref in enumerate((w_in_t, w_out_t, w_out, w_in))
    ]

    @pl.when(moved[0] == 1)
    def _():
        pltpu.make_async_copy(grad_got, b_grad, grad_sem.at[0]).start()

    @pl.when(moved[0] == 0)
    def _():
        pltpu.make_async_copy(grad_own, b_grad, grad_sem.at[0]).start()

    depth, rows = summed.shape
    pairs = {
        "normed": (b_normed, normed),
        "active": (b_active, active),
        "dsecond_low": (b_dsecond_low, dsecond_low),
        "dhidden": (b_dhidden, dhidden),
        "dsummed": (b_dsummed, dsummed),
    }

    def done(name, part):
        moves.emit(*pairs[name], part)
        if name == "active" and part.start == 0:
            moves.post_half(b_normed, normed_send, place)
        if name == "dhidden" and part.start == 0:
            moves.post_half(b_dsecond_low, dsecond_send, place)

    inv_s, mean, inv_2 = forward_part(
        inputs, holds.at[0], holds.at[1], waits[:2], b_normed, b_active, derivative, summed, second, done
    )
    for part in pieces(0, depth, STEP):
        second[part, :] = (second[part, :] - mean) * inv_2
    pltpu.make_async_copy(grad_own, b_grad, grad_sem.at[0]).wait()
    backward_part(
        lambda part: second[part, :], lambda part: b_grad[part, :].astype(F32), inv_2, inv_s,
        holds.at[2], holds.at[3], waits[2:], b_normed, derivative, b_dsecond_low, b_dhidden, b_dsummed, dsecond, done,
    )
    moves.finish()


def backward_kernel(number, place, carried, returned, following, normed, derivative, inverse_s, inverse_2, w_in, w_out,
                    dsecond_low, dhidden, dsummed, dsecond_send,
                    b_carried, b_returned, b_following, b_normed, b_derivative, b_inverse_s, b_inverse_2, holds,
                    b_dsecond_low, b_dhidden, b_dsummed, dsecond, sems):
    moves = copies(sems)
    first = (
        moves.fetch(carried, b_carried) + moves.fetch(returned, b_returned) + moves.fetch(following, b_following)
        + moves.fetch(inverse_s, b_inverse_s, 8) + moves.fetch(inverse_2, b_inverse_2, 8)
    )
    waits = [moves.fetch(w_out.at[number], holds.at[0])]
    early = moves.fetch(derivative, b_derivative) + moves.fetch(normed, b_normed)
    waits.append(moves.fetch(w_in.at[number], holds.at[1]))
    pairs = {
        "dsecond_low": (b_dsecond_low, dsecond_low),
        "dhidden": (b_dhidden, dhidden),
        "dsummed": (b_dsummed, dsummed),
    }

    def done(name, part):
        moves.emit(*pairs[name], part)
        if name == "dhidden" and part.start == 0:
            moves.post_half(b_dsecond_low, dsecond_send, place)

    def read_up(part):
        value = b_carried[part, :].astype(F32) + b_returned[part, :].astype(F32)
        return value.astype(BF).astype(F32)

    for copy in first + early:
        copy.wait()
    backward_part(
        lambda part: b_following[part, :].astype(F32), read_up, b_inverse_2[0:1, :], b_inverse_s[0:1, :],
        holds.at[0], holds.at[1], waits, b_normed, b_derivative, b_dsecond_low, b_dhidden, b_dsummed, dsecond, done,
    )
    moves.finish()


def grads_kernel(place, normed, dhidden, active, dsecond_low, normed_got, dhidden_got, active_got, dsecond_got,
                 sum_in, sum_out, b_normed, b_dhidden, b_active, b_dsecond_low, b_in, b_out, sems):
    moves = copies(sems)
    half = normed_got.shape[0]
    own = pl.ds(pl.multiple_of(place[0] * half, half), half)
    first = [moves.start(normed.at[own, :], b_normed.at[0]), moves.start(dhidden, b_dhidden.at[0])]
    first += [moves.start(normed_got, b_normed.at[1]), moves.start(dhidden_got, b_dhidden.at[1])]
    then = [moves.start(dsecond_low.at[own, :], b_dsecond_low.at[0]), moves.start(active, b_active.at[0])]
    then += [moves.start(dsecond_got, b_dsecond_low.at[1]), moves.start(active_got, b_active.at[1])]
    for copy in first:
        copy.wait()
    for part in pieces(0, half, CHUNK):
        term = nt(b_normed[0, part, :], b_dhidden[0]) + nt(b_normed[1, part, :], b_dhidden[1])
        b_in[part, :] = term.astype(BF)
        moves.emit(b_in, sum_in, part)
    for copy in then:
        copy.wait()
    for part in pieces(0, active.shape[0], CHUNK):
        term = nt(b_active[0, part, :], b_dsecond_low[0]) + nt(b_active[1, part, :], b_dsecond_low[1])
        b_out[part, :] = term.astype(BF)
        moves.emit(b_out, sum_out, part)
    moves.finish()


def weights_kernel(place, in_own, in_got, out_own, out_got, w_in, w_out, w_in_t, w_out_t):
    @pl.when(place[0] == 1)
    def _():
        w_in[...] = in_got[...]
        w_out[...] = out_got[...]

    @pl.when(place[0] == 0)
    def _():
        w_in[...] = in_own[...]
        w_out[...] = out_own[...]

    w_in_t[0] = w_in[0].T
    w_out_t[0] = w_out[0].T


def launch(kernel, outs, scratch, work, scalars, *operands):
    return pl.pallas_call(
        kernel,
        out_shape=[jax.ShapeDtypeStruct(shape, dtype) for shape, dtype in outs],
        in_specs=[SMEM] * scalars + [ANY] * (len(operands) - scalars),
        out_specs=[ANY] * len(outs),
        scratch_shapes=[pltpu.VMEM(*item) if isinstance(item, tuple) else pltpu.SemaphoreType.DMA((item,))
                        for item in scratch],
        compiler_params=pltpu.CompilerParams(vmem_limit_bytes=GRANT),
        cost_estimate=pl.CostEstimate(flops=0, bytes_accessed=work << 20, transcendentals=0),
    )(*operands)


SMEM = pl.BlockSpec(memory_space=pltpu.SMEM)
ANY = pl.BlockSpec(memory_space=pl.ANY)


def pick_weights(moved, in_own, in_got, out_own, out_got):
    blocks, depth, width = in_own.shape
    spec = pl.BlockSpec((1, depth, width), lambda k: (k, 0, 0))
    out = jax.ShapeDtypeStruct(in_own.shape, BF)
    return pl.pallas_call(
        weights_kernel,
        grid=(blocks,),
        out_shape=[out] * 4,
        in_specs=[SMEM] + [spec] * 4,
        out_specs=[spec] * 4,
        compiler_params=pltpu.CompilerParams(vmem_limit_bytes=GRANT),
        cost_estimate=pl.CostEstimate(flops=0, bytes_accessed=32 << 20, transcendentals=0),
    )(moved, in_own, in_got, out_own, out_got)


def grads(core, normed, dhidden, active, dsecond_low, *got):
    depth, rows = normed.shape
    width = active.shape[0]
    half = depth // 2
    outs = [((half, width), BF), ((width, half), BF)]
    scratch = [((2, half, rows), BF), ((2, width, rows), BF), ((2, width, rows), BF), ((2, half, rows), BF), *outs, 40]
    return launch(grads_kernel, outs, scratch, 10, 1, core, normed, dhidden, active, dsecond_low, *got)


def run_forward(number, core, mixed, current, w_in_t, w_out_t):
    tall = mixed.shape
    depth, rows = tall
    width = w_in_t.shape[1]
    wide, line = (width, rows), (8, rows)
    outs = [(tall, BF), (wide, BF), (wide, BF), (tall, BF), (line, F32), (line, F32)]
    half = ((depth // 2, rows), BF)
    scratch = [(tall, BF), (tall, BF), ((width, depth), BF), ((depth, width), BF), *outs, (tall, F32), (tall, F32), 60]
    return launch(functools.partial(forward_kernel, number), outs + [half], scratch, 16, 1,
                core, mixed, current, w_in_t, w_out_t)


def run_turn(number, core, moved, mixed, current, grad_own, grad_got, w_in_t, w_out_t, w_in, w_out):
    tall = mixed.shape
    depth, rows = tall
    width = w_in_t.shape[1]
    wide = (width, rows)
    outs = [(tall, BF), (wide, BF), (tall, BF), (wide, BF), (tall, BF)]
    scratch = [(tall, BF)] * 3 + [((4, depth, width), BF), *outs, (wide, F32), (tall, F32), (tall, F32), (tall, F32),
                                  80, 1]
    return launch(functools.partial(turn_kernel, number), outs + [((depth // 2, rows), BF)] * 2, scratch, 24, 2,
                core, moved, mixed, current, grad_own, grad_got, w_in_t, w_out_t, w_in, w_out)


def run_backward(number, core, carried, returned, following, normed, derivative, inverse_s, inverse_2, w_in, w_out):
    tall = carried.shape
    depth, rows = tall
    width = w_in.shape[2]
    wide, line = (width, rows), (8, rows)
    outs = [(tall, BF), (wide, BF), (tall, BF)]
    scratch = [(tall, BF), (tall, BF), (tall, BF), (tall, BF), (wide, BF), (line, F32), (line, F32),
               ((2, width, depth), BF), *outs, (tall, F32), 60]
    return launch(functools.partial(backward_kernel, number), outs + [((depth // 2, rows), BF)], scratch, 16, 1,
                core, carried, returned, following, normed, derivative, inverse_s, inverse_2, w_in, w_out)


def per_device(row_input, out_grad, in_weight, out_weight):
    row_input, out_grad = row_input[0], out_grad[0]
    in_weight, out_weight = in_weight[:, 0], out_weight[:, 0]
    last = lax.axis_index("tok") % 2
    core = last.astype(jnp.int32).reshape(1)
    is_moved = last != lax.axis_index("dp")
    moved = is_moved.astype(jnp.int32).reshape(1)

    def chosen(got, own):
        return jnp.where(is_moved, got, own)

    current = permute(row_input, ACROSS + STAY)
    got_in = permute(in_weight, HAND)
    got_out = permute(out_weight, HAND)
    current, got_in, got_out, out_grad = lax.optimization_barrier((current, got_in, got_out, out_grad))
    mixed = mix(current)
    w_in, w_out, w_in_t, w_out_t = pick_weights(moved, in_weight, got_in, out_weight, got_out)
    grad_got = swap(out_grad)
    normed_0, active_0, derivative_0, following_0, inverse_s_0, inverse_2_0, normed_send_0 = run_forward(
        0, core, mixed, current, w_in_t, w_out_t
    )
    mixed = mix(following_0)
    normed_got_0, active_got_0 = other_core(normed_send_0), other_core(active_0)
    normed_1, active_1, dsecond_low_1, dhidden_1, dsummed_1, normed_send_1, dsecond_send_1 = run_turn(
        1, core, moved, mixed, following_0, out_grad, grad_got, w_in_t, w_out_t, w_in, w_out
    )
    returned = mix(dsummed_1)
    sums_1 = grads(core, normed_1, dhidden_1, active_1, dsecond_low_1,
                   *[other_core(value) for value in (normed_send_1, dhidden_1, active_1, dsecond_send_1)])
    swapped_1 = [swap(value) for value in sums_1]
    returned, _ = lax.optimization_barrier((returned, sums_1))
    dsecond_low_0, dhidden_0, dsummed_0, dsecond_send_0 = run_backward(
        0, core, dsummed_1, returned, following_0, normed_0, derivative_0, inverse_s_0, inverse_2_0, w_in, w_out
    )
    dsummed_0, swapped_1[0] = lax.optimization_barrier((dsummed_0, swapped_1[0]))
    returned = mix(dsummed_0)
    dsecond_low_0, swapped_1[1] = lax.optimization_barrier((dsecond_low_0, swapped_1[1]))
    sums_0 = grads(core, normed_0, dhidden_0, active_0, dsecond_low_0,
                   normed_got_0, other_core(dhidden_0), active_got_0, other_core(dsecond_send_0))
    swapped_0 = [swap(value) for value in sums_0]
    grad_rows = (dsummed_0.astype(F32) + returned.astype(F32)).astype(BF)
    grad_rows = chosen(swap(grad_rows), grad_rows)
    grad_in = chosen(jnp.stack([swapped_0[0], swapped_1[0]]), jnp.stack([sums_0[0], sums_1[0]]))
    grad_out = chosen(jnp.stack([swapped_0[1], swapped_1[1]]), jnp.stack([sums_0[1], sums_1[1]]))
    return grad_rows[None], grad_in[:, None], grad_out[:, None]


def solution(mesh):
    return jax.shard_map(
        per_device,
        mesh=mesh,
        in_specs=(
            P("tok", None, "dp"),
            P("tok", None, "dp"),
            P(None, "tok", None, None),
            P(None, "tok", None, None),
        ),
        out_specs=(P("tok", None, "dp"), P(None, "tok", "dp", None), P(None, "tok", None, "dp")),
        check_vma=False,
    )
```

```python
import collections
import functools

import jax
import jax.numpy as jnp
from jax import lax
from jax.experimental import pallas as pl
from jax.experimental.pallas import tpu as pltpu
from jax.sharding import PartitionSpec as P

epsilon = 1e-05
BF = jnp.bfloat16
F32 = jnp.float32
BOTH = ("dp", "tok")
GRANT = 63 << 20
STEP = 32
CHUNK = 512
TILE = 512
EDGE = 256


def permute(value, pairs):
    tokens = lax.axis_size("tok")
    table = [
        (dp * tokens + base + last, to_dp * tokens + base + to_last)
        for base in range(0, tokens, 2)
        for (dp, last), (to_dp, to_last) in pairs
    ]
    return lax.ppermute(value, BOTH, table)


ACROSS = (((0, 1), (1, 0)), ((1, 0), (0, 1)))
STAY = (((0, 0), (0, 0)), ((1, 1), (1, 1)))
BESIDE = (((0, 0), (0, 1)), ((0, 1), (0, 0)), ((1, 0), (1, 1)), ((1, 1), (1, 0)))
HAND = (((0, 0), (0, 1)), ((1, 1), (1, 0)))


def swap(value):
    return permute(value, ACROSS)


def other_core(value):
    return permute(value, BESIDE)


def mix(value):
    tokens = lax.axis_size("tok")
    depth, rows = value.shape
    parts = value.reshape(tokens, depth // tokens, rows)
    groups = [
        [dp * tokens + base + last for base in range(0, tokens, 2) for dp in range(2)] for last in range(2)
    ]
    arrived = lax.all_to_all(
        parts, BOTH, split_axis=0, concat_axis=0, axis_index_groups=groups, tiled=True
    )
    return arrived.reshape(depth, rows)


def nn(left, right):
    return lax.dot_general(left, right, (((1,), (0,)), ((), ())), preferred_element_type=F32)


def nt(left, right):
    return lax.dot_general(left, right, (((1,), (1,)), ((), ())), preferred_element_type=F32)


def gelu_parts(hidden):
    cumulative = 0.5 * (1.0 + lax.erf(hidden * 0.7071067811865476))
    density = jnp.exp(-0.5 * hidden * hidden) * 0.3989422804014327
    return hidden * cumulative, cumulative + hidden * density


def fold(value):
    depth, rows = value.shape
    return jnp.sum(value.reshape(depth // 8, 8, rows), axis=0)


def total(value):
    return jnp.sum(value, axis=0, keepdims=True)


def pieces(start, stop, size):
    return [pl.ds(at, size) for at in range(start, stop, size)]


Moves = collections.namedtuple("Moves", ("start", "fetch", "emit", "post_half", "finish"))


def copies(sems):
    used, pending = [], []

    def start(source, target):
        copy = pltpu.make_async_copy(source, target, sems.at[len(used)])
        used.append(copy)
        copy.start()
        return copy

    def fetch(source, target, size=CHUNK):
        return [start(source.at[part, :], target.at[part, :]) for part in pieces(0, target.shape[0], size)]

    def emit(source, target, part):
        pending.append(start(source.at[part, :], target.at[part, :]))

    def post_half(source, target, place):
        half = target.shape[0]
        other = pl.ds(pl.multiple_of((1 - place[0]) * half, half), half)
        pending.append(start(source.at[other, :], target))

    def finish():
        for copy in pending:
            copy.wait()

    return Moves(start, fetch, emit, post_half, finish)


def norm_stats(values, depth, first):
    mean = total(first) * (1.0 / depth)
    second = jnp.zeros_like(first)
    for part in pieces(0, depth, STEP):
        center = values[part, :] - mean
        second += fold(center * center)
    return mean, lax.rsqrt(total(second) * (1.0 / depth) + epsilon)


def forward_part(inputs, w_in_t, w_out_t, waits, normed, active, derivative, summed, second, done):
    depth, rows = summed.shape
    mixed, current, mixed_waits, current_waits = inputs
    acc = jnp.zeros((8, rows), F32)
    for number, big in enumerate(range(0, depth, EDGE)):
        mixed_waits[number].wait()
        current_waits[number].wait()
        for part in pieces(big, big + EDGE, STEP):
            value = mixed[part, :].astype(F32) + current[part, :].astype(F32)
            summed[part, :] = value
            acc += fold(value)
    mean, inverse_s = norm_stats(summed, depth, acc)
    for big in range(0, depth, CHUNK):
        for part in pieces(big, big + CHUNK, STEP):
            normed[part, :] = ((summed[part, :] - mean) * inverse_s).astype(BF)
        done("normed", pl.ds(big, CHUNK))
    for copy in waits[0]:
        copy.wait()
    for big in range(0, w_in_t.shape[0], TILE):
        hidden = nn(w_in_t[pl.ds(big, TILE), :], normed[...])
        for small in range(0, TILE, STEP):
            act, der = gelu_parts(hidden[small : small + STEP])
            active[pl.ds(big + small, STEP), :] = act.astype(BF)
            derivative[pl.ds(big + small, STEP), :] = der.astype(derivative.dtype)
    for part in pieces(0, w_in_t.shape[0], CHUNK):
        done("active", part)
    acc = jnp.zeros((8, rows), F32)
    for copy in waits[1]:
        copy.wait()
    for big in range(0, depth, TILE):
        part = pl.ds(big, TILE)
        value = nn(w_out_t[part, :], active[...]) + normed[part, :].astype(F32)
        second[part, :] = value
        acc += fold(value)
    mean, inverse_2 = norm_stats(second, depth, acc)
    return inverse_s, mean, inverse_2


def forward_kernel(number, place, mixed, current, w_in_t, w_out_t, normed, active, derivative, following, inverse_s,
                   inverse_2, normed_send, b_mixed, b_current, b_in, b_out, b_normed, b_active, b_derivative, b_following,
                   b_inverse_s, b_inverse_2, summed, second, sems):
    moves = copies(sems)
    inputs = (b_mixed, b_current, moves.fetch(mixed, b_mixed, EDGE), moves.fetch(current, b_current, EDGE))
    waits = (moves.fetch(w_in_t.at[number], b_in), moves.fetch(w_out_t.at[number], b_out))
    depth, rows = summed.shape

    def done(name, part):
        if name == "normed":
            moves.emit(b_normed, normed, part)
        else:
            moves.emit(b_active, active, part)
            moves.emit(b_derivative, derivative, part)
        if name == "active" and part.start == 0:
            moves.post_half(b_normed, normed_send, place)

    inv_s, mean, inv_2 = forward_part(
        inputs, b_in, b_out, waits, b_normed, b_active, b_derivative, summed, second, done
    )
    b_inverse_s[...] = jnp.broadcast_to(inv_s, (8, rows))
    b_inverse_2[...] = jnp.broadcast_to(inv_2, (8, rows))
    moves.emit(b_inverse_s, inverse_s, pl.ds(0, 8))
    moves.emit(b_inverse_2, inverse_2, pl.ds(0, 8))
    for big in range(0, depth, EDGE):
        for part in pieces(big, big + EDGE, STEP):
            b_following[part, :] = ((second[part, :] - mean) * inv_2).astype(BF)
        moves.emit(b_following, following, pl.ds(big, EDGE))
    moves.finish()


def backward_part(read_hat, read_up, inverse_2, inverse_s, w_out, w_in, waits, normed, derivative,
                  dsecond_low, dhidden, dsummed, dsecond, done):
    depth, rows = normed.shape
    up_acc = jnp.zeros((8, rows), F32)
    cross_acc = jnp.zeros((8, rows), F32)
    for part in pieces(0, depth, STEP):
        upward = read_up(part)
        up_acc += fold(upward)
        cross_acc += fold(upward * read_hat(part))
    mean_up = total(up_acc) * (1.0 / depth)
    mean_cross = total(cross_acc) * (1.0 / depth)
    for big in range(0, depth, CHUNK):
        for part in pieces(big, big + CHUNK, STEP):
            value = inverse_2 * (read_up(part) - mean_up - read_hat(part) * mean_cross)
            dsecond[part, :] = value
            dsecond_low[part, :] = value.astype(BF)
        done("dsecond_low", pl.ds(big, CHUNK))
    for copy in waits[0]:
        copy.wait()
    for part in pieces(0, w_out.shape[0], TILE):
        value = nn(w_out[part, :], dsecond_low[...])
        dhidden[part, :] = (value * derivative[part, :].astype(F32)).astype(BF)
    for part in pieces(0, w_out.shape[0], CHUNK):
        done("dhidden", part)
    up_acc = jnp.zeros((8, rows), F32)
    cross_acc = jnp.zeros((8, rows), F32)
    for copy in waits[1]:
        copy.wait()
    for part in pieces(0, depth, TILE):
        value = nn(w_in[part, :], dhidden[...]) + dsecond[part, :]
        dsecond[part, :] = value
        up_acc += fold(value)
        cross_acc += fold(value * normed[part, :].astype(F32))
    mean_up = total(up_acc) * (1.0 / depth)
    mean_cross = total(cross_acc) * (1.0 / depth)
    for big in range(0, depth, EDGE):
        for part in pieces(big, big + EDGE, STEP):
            value = inverse_s * (dsecond[part, :] - mean_up - normed[part, :].astype(F32) * mean_cross)
            dsummed[part, :] = value.astype(BF)
        done("dsummed", pl.ds(big, EDGE))


def turn_kernel(number, place, moved, mixed, current, grad_own, grad_got, w_in_t, w_out_t, w_in, w_out,
                normed, active, dsecond_low, dhidden, dsummed, normed_send, dsecond_send,
                b_mixed, b_current, b_grad, holds, b_normed, b_active, b_dsecond_low, b_dhidden, b_dsummed,
                derivative, summed, second, dsecond, sems, grad_sem):
    moves = copies(sems)
    inputs = (b_mixed, b_current, moves.fetch(mixed, b_mixed, EDGE), moves.fetch(current, b_current, EDGE))
    waits = [
        moves.fetch(ref.at[number], holds.at[at]) for at, ref in enumerate((w_in_t, w_out_t, w_out, w_in))
    ]

    @pl.when(moved[0] == 1)
    def _():
        pltpu.make_async_copy(grad_got, b_grad, grad_sem.at[0]).start()

    @pl.when(moved[0] == 0)
    def _():
        pltpu.make_async_copy(grad_own, b_grad, grad_sem.at[0]).start()

    depth, rows = summed.shape
    pairs = {
        "normed": (b_normed, normed),
        "active": (b_active, active),
        "dsecond_low": (b_dsecond_low, dsecond_low),
        "dhidden": (b_dhidden, dhidden),
        "dsummed": (b_dsummed, dsummed),
    }

    def done(name, part):
        moves.emit(*pairs[name], part)
        if name == "active" and part.start == 0:
            moves.post_half(b_normed, normed_send, place)
        if name == "dhidden" and part.start == 0:
            moves.post_half(b_dsecond_low, dsecond_send, place)

    inv_s, mean, inv_2 = forward_part(
        inputs, holds.at[0], holds.at[1], waits[:2], b_normed, b_active, derivative, summed, second, done
    )
    for part in pieces(0, depth, STEP):
        second[part, :] = (second[part, :] - mean) * inv_2
    pltpu.make_async_copy(grad_own, b_grad, grad_sem.at[0]).wait()
    backward_part(
        lambda part: second[part, :], lambda part: b_grad[part, :].astype(F32), inv_2, inv_s,
        holds.at[2], holds.at[3], waits[2:], b_normed, derivative, b_dsecond_low, b_dhidden, b_dsummed, dsecond, done,
    )
    moves.finish()


def backward_kernel(number, place, carried, returned, following, normed, derivative, inverse_s, inverse_2, w_in, w_out,
                    dsecond_low, dhidden, dsummed, dsecond_send,
                    b_carried, b_returned, b_following, b_normed, b_derivative, b_inverse_s, b_inverse_2, holds,
                    b_dsecond_low, b_dhidden, b_dsummed, dsecond, sems):
    moves = copies(sems)
    first = (
        moves.fetch(carried, b_carried) + moves.fetch(returned, b_returned) + moves.fetch(following, b_following)
        + moves.fetch(inverse_s, b_inverse_s, 8) + moves.fetch(inverse_2, b_inverse_2, 8)
    )
    waits = [moves.fetch(w_out.at[number], holds.at[0])]
    early = moves.fetch(derivative, b_derivative) + moves.fetch(normed, b_normed)
    waits.append(moves.fetch(w_in.at[number], holds.at[1]))
    pairs = {
        "dsecond_low": (b_dsecond_low, dsecond_low),
        "dhidden": (b_dhidden, dhidden),
        "dsummed": (b_dsummed, dsummed),
    }

    def done(name, part):
        moves.emit(*pairs[name], part)
        if name == "dhidden" and part.start == 0:
            moves.post_half(b_dsecond_low, dsecond_send, place)

    def read_up(part):
        value = b_carried[part, :].astype(F32) + b_returned[part, :].astype(F32)
        return value.astype(BF).astype(F32)

    for copy in first + early:
        copy.wait()
    backward_part(
        lambda part: b_following[part, :].astype(F32), read_up, b_inverse_2[0:1, :], b_inverse_s[0:1, :],
        holds.at[0], holds.at[1], waits, b_normed, b_derivative, b_dsecond_low, b_dhidden, b_dsummed, dsecond, done,
    )
    moves.finish()


def grads_kernel(place, normed, dhidden, active, dsecond_low, normed_got, dhidden_got, active_got, dsecond_got,
                 sum_in, sum_out, b_normed, b_dhidden, b_active, b_dsecond_low, b_in, b_out, sems):
    moves = copies(sems)
    half = normed_got.shape[0]
    own = pl.ds(pl.multiple_of(place[0] * half, half), half)
    first = [moves.start(normed.at[own, :], b_normed.at[0]), moves.start(dhidden, b_dhidden.at[0])]
    first += [moves.start(normed_got, b_normed.at[1]), moves.start(dhidden_got, b_dhidden.at[1])]
    then = [moves.start(dsecond_low.at[own, :], b_dsecond_low.at[0]), moves.start(active, b_active.at[0])]
    then += [moves.start(dsecond_got, b_dsecond_low.at[1]), moves.start(active_got, b_active.at[1])]
    for copy in first:
        copy.wait()
    for part in pieces(0, half, CHUNK):
        term = nt(b_normed[0, part, :], b_dhidden[0]) + nt(b_normed[1, part, :], b_dhidden[1])
        b_in[part, :] = term.astype(BF)
        moves.emit(b_in, sum_in, part)
    for copy in then:
        copy.wait()
    for part in pieces(0, active.shape[0], CHUNK):
        term = nt(b_active[0, part, :], b_dsecond_low[0]) + nt(b_active[1, part, :], b_dsecond_low[1])
        b_out[part, :] = term.astype(BF)
        moves.emit(b_out, sum_out, part)
    moves.finish()


def weights_kernel(place, in_own, in_got, out_own, out_got, w_in, w_out, w_in_t, w_out_t):
    @pl.when(place[0] == 1)
    def _():
        w_in[...] = in_got[...]
        w_out[...] = out_got[...]

    @pl.when(place[0] == 0)
    def _():
        w_in[...] = in_own[...]
        w_out[...] = out_own[...]

    w_in_t[0] = w_in[0].T
    w_out_t[0] = w_out[0].T


def launch(kernel, outs, scratch, work, scalars, *operands):
    return pl.pallas_call(
        kernel,
        out_shape=[jax.ShapeDtypeStruct(shape, dtype) for shape, dtype in outs],
        in_specs=[SMEM] * scalars + [ANY] * (len(operands) - scalars),
        out_specs=[ANY] * len(outs),
        scratch_shapes=[pltpu.VMEM(*item) if isinstance(item, tuple) else pltpu.SemaphoreType.DMA((item,))
                        for item in scratch],
        compiler_params=pltpu.CompilerParams(vmem_limit_bytes=GRANT),
        cost_estimate=pl.CostEstimate(flops=0, bytes_accessed=work << 20, transcendentals=0),
    )(*operands)


SMEM = pl.BlockSpec(memory_space=pltpu.SMEM)
ANY = pl.BlockSpec(memory_space=pl.ANY)


def pick_weights(moved, in_own, in_got, out_own, out_got):
    blocks, depth, width = in_own.shape
    spec = pl.BlockSpec((1, depth, width), lambda k: (k, 0, 0))
    out = jax.ShapeDtypeStruct(in_own.shape, BF)
    return pl.pallas_call(
        weights_kernel,
        grid=(blocks,),
        out_shape=[out] * 4,
        in_specs=[SMEM] + [spec] * 4,
        out_specs=[spec] * 4,
        compiler_params=pltpu.CompilerParams(vmem_limit_bytes=GRANT),
        cost_estimate=pl.CostEstimate(flops=0, bytes_accessed=32 << 20, transcendentals=0),
    )(moved, in_own, in_got, out_own, out_got)


def grads(core, normed, dhidden, active, dsecond_low, *got):
    depth, rows = normed.shape
    width = active.shape[0]
    half = depth // 2
    outs = [((half, width), BF), ((width, half), BF)]
    scratch = [((2, half, rows), BF), ((2, width, rows), BF), ((2, width, rows), BF), ((2, half, rows), BF), *outs, 40]
    return launch(grads_kernel, outs, scratch, 10, 1, core, normed, dhidden, active, dsecond_low, *got)


def run_forward(number, core, mixed, current, w_in_t, w_out_t):
    tall = mixed.shape
    depth, rows = tall
    width = w_in_t.shape[1]
    wide, line = (width, rows), (8, rows)
    outs = [(tall, BF), (wide, BF), (wide, BF), (tall, BF), (line, F32), (line, F32)]
    half = ((depth // 2, rows), BF)
    scratch = [(tall, BF), (tall, BF), ((width, depth), BF), ((depth, width), BF), *outs, (tall, F32), (tall, F32), 60]
    return launch(functools.partial(forward_kernel, number), outs + [half], scratch, 16, 1,
                core, mixed, current, w_in_t, w_out_t)


def run_turn(number, core, moved, mixed, current, grad_own, grad_got, w_in_t, w_out_t, w_in, w_out):
    tall = mixed.shape
    depth, rows = tall
    width = w_in_t.shape[1]
    wide = (width, rows)
    outs = [(tall, BF), (wide, BF), (tall, BF), (wide, BF), (tall, BF)]
    scratch = [(tall, BF)] * 3 + [((4, depth, width), BF), *outs, (wide, F32), (tall, F32), (tall, F32), (tall, F32),
                                  80, 1]
    return launch(functools.partial(turn_kernel, number), outs + [((depth // 2, rows), BF)] * 2, scratch, 24, 2,
                core, moved, mixed, current, grad_own, grad_got, w_in_t, w_out_t, w_in, w_out)


def run_backward(number, core, carried, returned, following, normed, derivative, inverse_s, inverse_2, w_in, w_out):
    tall = carried.shape
    depth, rows = tall
    width = w_in.shape[2]
    wide, line = (width, rows), (8, rows)
    outs = [(tall, BF), (wide, BF), (tall, BF)]
    scratch = [(tall, BF), (tall, BF), (tall, BF), (tall, BF), (wide, BF), (line, F32), (line, F32),
               ((2, width, depth), BF), *outs, (tall, F32), 60]
    return launch(functools.partial(backward_kernel, number), outs + [((depth // 2, rows), BF)], scratch, 16, 1,
                core, carried, returned, following, normed, derivative, inverse_s, inverse_2, w_in, w_out)


def per_device(row_input, out_grad, in_weight, out_weight):
    row_input, out_grad = row_input[0], out_grad[0]
    in_weight, out_weight = in_weight[:, 0], out_weight[:, 0]
    last = lax.axis_index("tok") % 2
    core = last.astype(jnp.int32).reshape(1)
    is_moved = last != lax.axis_index("dp")
    moved = is_moved.astype(jnp.int32).reshape(1)

    def chosen(got, own):
        return jnp.where(is_moved, got, own)

    current = permute(row_input, ACROSS + STAY)
    got_in = permute(in_weight, HAND)
    got_out = permute(out_weight, HAND)
    current, got_in, got_out = lax.optimization_barrier((current, got_in, got_out))
    mixed = mix(current)
    w_in, w_out, w_in_t, w_out_t = pick_weights(moved, in_weight, got_in, out_weight, got_out)
    w_in_t, out_grad = lax.optimization_barrier((w_in_t, out_grad))
    grad_got = swap(out_grad)
    normed_0, active_0, derivative_0, following_0, inverse_s_0, inverse_2_0, normed_send_0 = run_forward(
        0, core, mixed, current, w_in_t, w_out_t
    )
    mixed = mix(following_0)
    normed_got_0, active_got_0 = other_core(normed_send_0), other_core(active_0)
    normed_1, active_1, dsecond_low_1, dhidden_1, dsummed_1, normed_send_1, dsecond_send_1 = run_turn(
        1, core, moved, mixed, following_0, out_grad, grad_got, w_in_t, w_out_t, w_in, w_out
    )
    returned = mix(dsummed_1)
    sums_1 = grads(core, normed_1, dhidden_1, active_1, dsecond_low_1,
                   *[other_core(value) for value in (normed_send_1, dhidden_1, active_1, dsecond_send_1)])
    swapped_1 = [swap(value) for value in sums_1]
    returned, _ = lax.optimization_barrier((returned, sums_1))
    dsecond_low_0, dhidden_0, dsummed_0, dsecond_send_0 = run_backward(
        0, core, dsummed_1, returned, following_0, normed_0, derivative_0, inverse_s_0, inverse_2_0, w_in, w_out
    )
    dsummed_0, swapped_1[0] = lax.optimization_barrier((dsummed_0, swapped_1[0]))
    returned = mix(dsummed_0)
    dsecond_low_0, swapped_1[1] = lax.optimization_barrier((dsecond_low_0, swapped_1[1]))
    sums_0 = grads(core, normed_0, dhidden_0, active_0, dsecond_low_0,
                   normed_got_0, other_core(dhidden_0), active_got_0, other_core(dsecond_send_0))
    swapped_0 = [swap(value) for value in sums_0]
    grad_rows = (dsummed_0.astype(F32) + returned.astype(F32)).astype(BF)
    grad_rows = chosen(swap(grad_rows), grad_rows)
    grad_in = chosen(jnp.stack([swapped_0[0], swapped_1[0]]), jnp.stack([sums_0[0], sums_1[0]]))
    grad_out = chosen(jnp.stack([swapped_0[1], swapped_1[1]]), jnp.stack([sums_0[1], sums_1[1]]))
    return grad_rows[None], grad_in[:, None], grad_out[:, None]


def solution(mesh):
    return jax.shard_map(
        per_device,
        mesh=mesh,
        in_specs=(
            P("tok", None, "dp"),
            P("tok", None, "dp"),
            P(None, "tok", None, None),
            P(None, "tok", None, None),
        ),
        out_specs=(P("tok", None, "dp"), P(None, "tok", "dp", None), P(None, "tok", None, "dp")),
        check_vma=False,
    )
```

```python
import collections
import functools

import jax
import jax.numpy as jnp
from jax import lax
from jax.experimental import pallas as pl
from jax.experimental.pallas import tpu as pltpu
from jax.sharding import PartitionSpec as P

epsilon = 1e-05
BF = jnp.bfloat16
F32 = jnp.float32
BOTH = ("dp", "tok")
GRANT = 63 << 20
STEP = 32
CHUNK = 512
TILE = 512
EDGE = 256


def permute(value, pairs):
    tokens = lax.axis_size("tok")
    table = [
        (dp * tokens + base + last, to_dp * tokens + base + to_last)
        for base in range(0, tokens, 2)
        for (dp, last), (to_dp, to_last) in pairs
    ]
    return lax.ppermute(value, BOTH, table)


ACROSS = (((0, 1), (1, 0)), ((1, 0), (0, 1)))
STAY = (((0, 0), (0, 0)), ((1, 1), (1, 1)))
BESIDE = (((0, 0), (0, 1)), ((0, 1), (0, 0)), ((1, 0), (1, 1)), ((1, 1), (1, 0)))
HAND = (((0, 0), (0, 1)), ((1, 1), (1, 0)))


def swap(value):
    return permute(value, ACROSS)


def other_core(value):
    return permute(value, BESIDE)


def mix(value):
    tokens = lax.axis_size("tok")
    depth, rows = value.shape
    parts = value.reshape(tokens, depth // tokens, rows)
    groups = [
        [dp * tokens + base + last for base in range(0, tokens, 2) for dp in range(2)] for last in range(2)
    ]
    arrived = lax.all_to_all(
        parts, BOTH, split_axis=0, concat_axis=0, axis_index_groups=groups, tiled=True
    )
    return arrived.reshape(depth, rows)


def nn(left, right):
    return lax.dot_general(left, right, (((1,), (0,)), ((), ())), preferred_element_type=F32)


def nt(left, right):
    return lax.dot_general(left, right, (((1,), (1,)), ((), ())), preferred_element_type=F32)


def gelu_parts(hidden):
    cumulative = 0.5 * (1.0 + lax.erf(hidden * 0.7071067811865476))
    density = jnp.exp(-0.5 * hidden * hidden) * 0.3989422804014327
    return hidden * cumulative, cumulative + hidden * density


def fold(value):
    depth, rows = value.shape
    return jnp.sum(value.reshape(depth // 8, 8, rows), axis=0)


def total(value):
    return jnp.sum(value, axis=0, keepdims=True)


def pieces(start, stop, size):
    return [pl.ds(at, size) for at in range(start, stop, size)]


Moves = collections.namedtuple("Moves", ("start", "fetch", "emit", "post_half", "finish"))


def copies(sems):
    used, pending = [], []

    def start(source, target):
        copy = pltpu.make_async_copy(source, target, sems.at[len(used)])
        used.append(copy)
        copy.start()
        return copy

    def fetch(source, target, size=CHUNK):
        return [start(source.at[part, :], target.at[part, :]) for part in pieces(0, target.shape[0], size)]

    def emit(source, target, part):
        pending.append(start(source.at[part, :], target.at[part, :]))

    def post_half(source, target, place):
        half = target.shape[0]
        other = pl.ds(pl.multiple_of((1 - place[0]) * half, half), half)
        pending.append(start(source.at[other, :], target))

    def finish():
        for copy in pending:
            copy.wait()

    return Moves(start, fetch, emit, post_half, finish)


def norm_stats(values, depth, first):
    mean = total(first) * (1.0 / depth)
    second = jnp.zeros_like(first)
    for part in pieces(0, depth, STEP):
        center = values[part, :] - mean
        second += fold(center * center)
    return mean, lax.rsqrt(total(second) * (1.0 / depth) + epsilon)


def forward_part(inputs, w_in_t, w_out_t, waits, normed, active, derivative, summed, second, done):
    depth, rows = summed.shape
    mixed, current, mixed_waits, current_waits = inputs
    acc = jnp.zeros((8, rows), F32)
    for number, big in enumerate(range(0, depth, EDGE)):
        mixed_waits[number].wait()
        current_waits[number].wait()
        for part in pieces(big, big + EDGE, STEP):
            value = mixed[part, :].astype(F32) + current[part, :].astype(F32)
            summed[part, :] = value
            acc += fold(value)
    mean, inverse_s = norm_stats(summed, depth, acc)
    for big in range(0, depth, CHUNK):
        for part in pieces(big, big + CHUNK, STEP):
            normed[part, :] = ((summed[part, :] - mean) * inverse_s).astype(BF)
        done("normed", pl.ds(big, CHUNK))
    for copy in waits[0]:
        copy.wait()
    for big in range(0, w_in_t.shape[0], TILE):
        hidden = nn(w_in_t[pl.ds(big, TILE), :], normed[...])
        for small in range(0, TILE, STEP):
            act, der = gelu_parts(hidden[small : small + STEP])
            active[pl.ds(big + small, STEP), :] = act.astype(BF)
            derivative[pl.ds(big + small, STEP), :] = der.astype(derivative.dtype)
    for part in pieces(0, w_in_t.shape[0], CHUNK):
        done("active", part)
    acc = jnp.zeros((8, rows), F32)
    for copy in waits[1]:
        copy.wait()
    for big in range(0, depth, TILE):
        part = pl.ds(big, TILE)
        value = nn(w_out_t[part, :], active[...]) + normed[part, :].astype(F32)
        second[part, :] = value
        acc += fold(value)
    mean, inverse_2 = norm_stats(second, depth, acc)
    return inverse_s, mean, inverse_2


def forward_kernel(number, place, mixed, current, w_in_t, w_out_t, normed, active, derivative, following, inverse_s,
                   inverse_2, normed_send, b_mixed, b_current, b_in, b_out, b_normed, b_active, b_derivative, b_following,
                   b_inverse_s, b_inverse_2, summed, second, sems):
    moves = copies(sems)
    inputs = (b_mixed, b_current, moves.fetch(mixed, b_mixed, EDGE), moves.fetch(current, b_current, EDGE))
    waits = (moves.fetch(w_in_t.at[number], b_in), moves.fetch(w_out_t.at[number], b_out))
    depth, rows = summed.shape

    def done(name, part):
        if name == "normed":
            moves.emit(b_normed, normed, part)
        else:
            moves.emit(b_active, active, part)
            moves.emit(b_derivative, derivative, part)
        if name == "active" and part.start == 0:
            moves.post_half(b_normed, normed_send, place)

    inv_s, mean, inv_2 = forward_part(
        inputs, b_in, b_out, waits, b_normed, b_active, b_derivative, summed, second, done
    )
    b_inverse_s[...] = jnp.broadcast_to(inv_s, (8, rows))
    b_inverse_2[...] = jnp.broadcast_to(inv_2, (8, rows))
    moves.emit(b_inverse_s, inverse_s, pl.ds(0, 8))
    moves.emit(b_inverse_2, inverse_2, pl.ds(0, 8))
    for big in range(0, depth, EDGE):
        for part in pieces(big, big + EDGE, STEP):
            b_following[part, :] = ((second[part, :] - mean) * inv_2).astype(BF)
        moves.emit(b_following, following, pl.ds(big, EDGE))
    moves.finish()


def backward_part(read_hat, read_up, inverse_2, inverse_s, w_out, w_in, waits, normed, derivative,
                  dsecond_low, dhidden, dsummed, dsecond, done):
    depth, rows = normed.shape
    up_acc = jnp.zeros((8, rows), F32)
    cross_acc = jnp.zeros((8, rows), F32)
    for part in pieces(0, depth, STEP):
        upward = read_up(part)
        up_acc += fold(upward)
        cross_acc += fold(upward * read_hat(part))
    mean_up = total(up_acc) * (1.0 / depth)
    mean_cross = total(cross_acc) * (1.0 / depth)
    for big in range(0, depth, CHUNK):
        for part in pieces(big, big + CHUNK, STEP):
            value = inverse_2 * (read_up(part) - mean_up - read_hat(part) * mean_cross)
            dsecond[part, :] = value
            dsecond_low[part, :] = value.astype(BF)
        done("dsecond_low", pl.ds(big, CHUNK))
    for copy in waits[0]:
        copy.wait()
    for part in pieces(0, w_out.shape[0], TILE):
        value = nn(w_out[part, :], dsecond_low[...])
        dhidden[part, :] = (value * derivative[part, :].astype(F32)).astype(BF)
    for part in pieces(0, w_out.shape[0], CHUNK):
        done("dhidden", part)
    up_acc = jnp.zeros((8, rows), F32)
    cross_acc = jnp.zeros((8, rows), F32)
    for copy in waits[1]:
        copy.wait()
    for part in pieces(0, depth, TILE):
        value = nn(w_in[part, :], dhidden[...]) + dsecond[part, :]
        dsecond[part, :] = value
        up_acc += fold(value)
        cross_acc += fold(value * normed[part, :].astype(F32))
    mean_up = total(up_acc) * (1.0 / depth)
    mean_cross = total(cross_acc) * (1.0 / depth)
    for big in range(0, depth, EDGE):
        for part in pieces(big, big + EDGE, STEP):
            value = inverse_s * (dsecond[part, :] - mean_up - normed[part, :].astype(F32) * mean_cross)
            dsummed[part, :] = value.astype(BF)
        done("dsummed", pl.ds(big, EDGE))


def turn_kernel(number, place, moved, mixed, current, grad_own, grad_got, w_in_t, w_out_t, w_in, w_out,
                normed, active, dsecond_low, dhidden, dsummed, halves_send,
                b_mixed, b_current, b_grad, holds, b_normed, b_active, b_dsecond_low, b_dhidden, b_dsummed,
                derivative, summed, second, dsecond, sems, grad_sem):
    moves = copies(sems)
    inputs = (b_mixed, b_current, moves.fetch(mixed, b_mixed, EDGE), moves.fetch(current, b_current, EDGE))
    waits = [
        moves.fetch(ref.at[number], holds.at[at]) for at, ref in enumerate((w_in_t, w_out_t, w_out, w_in))
    ]

    @pl.when(moved[0] == 1)
    def _():
        pltpu.make_async_copy(grad_got, b_grad, grad_sem.at[0]).start()

    @pl.when(moved[0] == 0)
    def _():
        pltpu.make_async_copy(grad_own, b_grad, grad_sem.at[0]).start()

    depth, rows = summed.shape
    pairs = {
        "normed": (b_normed, normed),
        "active": (b_active, active),
        "dsecond_low": (b_dsecond_low, dsecond_low),
        "dhidden": (b_dhidden, dhidden),
        "dsummed": (b_dsummed, dsummed),
    }

    def done(name, part):
        moves.emit(*pairs[name], part)
        if name == "active" and part.start == 0:
            moves.post_half(b_normed, halves_send.at[pl.ds(0, depth // 2), :], place)
        if name == "dhidden" and part.start == 0:
            moves.post_half(b_dsecond_low, halves_send.at[pl.ds(depth // 2, depth // 2), :], place)

    inv_s, mean, inv_2 = forward_part(
        inputs, holds.at[0], holds.at[1], waits[:2], b_normed, b_active, derivative, summed, second, done
    )
    pltpu.make_async_copy(grad_own, b_grad, grad_sem.at[0]).wait()
    backward_part(
        lambda part: (second[part, :] - mean) * inv_2, lambda part: b_grad[part, :].astype(F32), inv_2, inv_s,
        holds.at[2], holds.at[3], waits[2:], b_normed, derivative, b_dsecond_low, b_dhidden, b_dsummed, dsecond, done,
    )
    moves.finish()


def backward_kernel(number, place, carried, returned, following, normed, derivative, inverse_s, inverse_2, w_in, w_out,
                    dsecond_low, dhidden, dsummed, dsecond_send,
                    b_carried, b_returned, b_following, b_normed, b_derivative, b_inverse_s, b_inverse_2, holds,
                    b_dsecond_low, b_dhidden, b_dsummed, dsecond, sems):
    moves = copies(sems)
    first = (
        moves.fetch(carried, b_carried) + moves.fetch(returned, b_returned) + moves.fetch(following, b_following)
        + moves.fetch(inverse_s, b_inverse_s, 8) + moves.fetch(inverse_2, b_inverse_2, 8)
    )
    waits = [moves.fetch(w_out.at[number], holds.at[0])]
    early = moves.fetch(derivative, b_derivative) + moves.fetch(normed, b_normed)
    waits.append(moves.fetch(w_in.at[number], holds.at[1]))
    pairs = {
        "dsecond_low": (b_dsecond_low, dsecond_low),
        "dhidden": (b_dhidden, dhidden),
        "dsummed": (b_dsummed, dsummed),
    }

    def done(name, part):
        moves.emit(*pairs[name], part)
        if name == "dhidden" and part.start == 0:
            moves.post_half(b_dsecond_low, dsecond_send, place)

    def read_up(part):
        value = b_carried[part, :].astype(F32) + b_returned[part, :].astype(F32)
        return value.astype(BF).astype(F32)

    for copy in first + early:
        copy.wait()
    backward_part(
        lambda part: b_following[part, :].astype(F32), read_up, b_inverse_2[0:1, :], b_inverse_s[0:1, :],
        holds.at[0], holds.at[1], waits, b_normed, b_derivative, b_dsecond_low, b_dhidden, b_dsummed, dsecond, done,
    )
    moves.finish()


def grads_kernel(place, normed, dhidden, active, dsecond_low, normed_got, dhidden_got, active_got, dsecond_got,
                 sum_in, sum_out, b_normed, b_dhidden, b_active, b_dsecond_low, b_in, b_out, sems):
    moves = copies(sems)
    half = normed.shape[0] // 2
    late = pl.ds(dsecond_got.shape[0] - half, half)
    own = pl.ds(pl.multiple_of(place[0] * half, half), half)
    first = [moves.start(normed.at[own, :], b_normed.at[0]), moves.start(dhidden, b_dhidden.at[0])]
    first += [moves.start(normed_got.at[pl.ds(0, half), :], b_normed.at[1]), moves.start(dhidden_got, b_dhidden.at[1])]
    then = [moves.start(dsecond_low.at[own, :], b_dsecond_low.at[0]), moves.start(active, b_active.at[0])]
    then += [moves.start(dsecond_got.at[late, :], b_dsecond_low.at[1]), moves.start(active_got, b_active.at[1])]
    for copy in first:
        copy.wait()
    for part in pieces(0, half, CHUNK):
        term = nt(b_normed[0, part, :], b_dhidden[0]) + nt(b_normed[1, part, :], b_dhidden[1])
        b_in[part, :] = term.astype(BF)
        moves.emit(b_in, sum_in, part)
    for copy in then:
        copy.wait()
    for part in pieces(0, active.shape[0], CHUNK):
        term = nt(b_active[0, part, :], b_dsecond_low[0]) + nt(b_active[1, part, :], b_dsecond_low[1])
        b_out[part, :] = term.astype(BF)
        moves.emit(b_out, sum_out, part)
    moves.finish()


def weights_kernel(place, in_own, in_got, out_own, out_got, w_in, w_out, w_in_t, w_out_t):
    @pl.when(place[0] == 1)
    def _():
        w_in[...] = in_got[...]
        w_out[...] = out_got[...]

    @pl.when(place[0] == 0)
    def _():
        w_in[...] = in_own[...]
        w_out[...] = out_own[...]

    w_in_t[0] = w_in[0].T
    w_out_t[0] = w_out[0].T


def launch(kernel, outs, scratch, work, scalars, *operands):
    return pl.pallas_call(
        kernel,
        out_shape=[jax.ShapeDtypeStruct(shape, dtype) for shape, dtype in outs],
        in_specs=[SMEM] * scalars + [ANY] * (len(operands) - scalars),
        out_specs=[ANY] * len(outs),
        scratch_shapes=[pltpu.VMEM(*item) if isinstance(item, tuple) else pltpu.SemaphoreType.DMA((item,))
                        for item in scratch],
        compiler_params=pltpu.CompilerParams(vmem_limit_bytes=GRANT),
        cost_estimate=pl.CostEstimate(flops=0, bytes_accessed=work << 20, transcendentals=0),
    )(*operands)


SMEM = pl.BlockSpec(memory_space=pltpu.SMEM)
ANY = pl.BlockSpec(memory_space=pl.ANY)


def pick_weights(moved, in_own, in_got, out_own, out_got):
    blocks, depth, width = in_own.shape
    spec = pl.BlockSpec((1, depth, width), lambda k: (k, 0, 0))
    out = jax.ShapeDtypeStruct(in_own.shape, BF)
    return pl.pallas_call(
        weights_kernel,
        grid=(blocks,),
        out_shape=[out] * 4,
        in_specs=[SMEM] + [spec] * 4,
        out_specs=[spec] * 4,
        compiler_params=pltpu.CompilerParams(vmem_limit_bytes=GRANT),
        cost_estimate=pl.CostEstimate(flops=0, bytes_accessed=32 << 20, transcendentals=0),
    )(moved, in_own, in_got, out_own, out_got)


def grads(core, normed, dhidden, active, dsecond_low, *got):
    depth, rows = normed.shape
    width = active.shape[0]
    half = depth // 2
    outs = [((half, width), BF), ((width, half), BF)]
    scratch = [((2, half, rows), BF), ((2, width, rows), BF), ((2, width, rows), BF), ((2, half, rows), BF), *outs, 40]
    return launch(grads_kernel, outs, scratch, 10, 1, core, normed, dhidden, active, dsecond_low, *got)


def run_forward(number, core, mixed, current, w_in_t, w_out_t):
    tall = mixed.shape
    depth, rows = tall
    width = w_in_t.shape[1]
    wide, line = (width, rows), (8, rows)
    outs = [(tall, BF), (wide, BF), (wide, BF), (tall, BF), (line, F32), (line, F32)]
    half = ((depth // 2, rows), BF)
    scratch = [(tall, BF), (tall, BF), ((width, depth), BF), ((depth, width), BF), *outs, (tall, F32), (tall, F32), 60]
    return launch(functools.partial(forward_kernel, number), outs + [half], scratch, 16, 1,
                core, mixed, current, w_in_t, w_out_t)


def run_turn(number, core, moved, mixed, current, grad_own, grad_got, w_in_t, w_out_t, w_in, w_out):
    tall = mixed.shape
    depth, rows = tall
    width = w_in_t.shape[1]
    wide = (width, rows)
    outs = [(tall, BF), (wide, BF), (tall, BF), (wide, BF), (tall, BF)]
    scratch = [(tall, BF)] * 3 + [((4, depth, width), BF), *outs, (wide, F32), (tall, F32), (tall, F32), (tall, F32),
                                  80, 1]
    return launch(functools.partial(turn_kernel, number), outs + [(tall, BF)], scratch, 24, 2,
                core, moved, mixed, current, grad_own, grad_got, w_in_t, w_out_t, w_in, w_out)


def run_backward(number, core, carried, returned, following, normed, derivative, inverse_s, inverse_2, w_in, w_out):
    tall = carried.shape
    depth, rows = tall
    width = w_in.shape[2]
    wide, line = (width, rows), (8, rows)
    outs = [(tall, BF), (wide, BF), (tall, BF)]
    scratch = [(tall, BF), (tall, BF), (tall, BF), (tall, BF), (wide, BF), (line, F32), (line, F32),
               ((2, width, depth), BF), *outs, (tall, F32), 60]
    return launch(functools.partial(backward_kernel, number), outs + [((depth // 2, rows), BF)], scratch, 16, 1,
                core, carried, returned, following, normed, derivative, inverse_s, inverse_2, w_in, w_out)


def per_device(row_input, out_grad, in_weight, out_weight):
    row_input, out_grad = row_input[0], out_grad[0]
    in_weight, out_weight = in_weight[:, 0], out_weight[:, 0]
    last = lax.axis_index("tok") % 2
    core = last.astype(jnp.int32).reshape(1)
    is_moved = last != lax.axis_index("dp")
    moved = is_moved.astype(jnp.int32).reshape(1)

    def chosen(got, own):
        return jnp.where(is_moved, got, own)

    current = permute(row_input, ACROSS + STAY)
    got_in = permute(in_weight, HAND)
    got_out = permute(out_weight, HAND)
    current, got_in, got_out = lax.optimization_barrier((current, got_in, got_out))
    mixed = mix(current)
    w_in, w_out, w_in_t, w_out_t = pick_weights(moved, in_weight, got_in, out_weight, got_out)
    w_in_t, out_grad = lax.optimization_barrier((w_in_t, out_grad))
    grad_got = swap(out_grad)
    normed_0, active_0, derivative_0, following_0, inverse_s_0, inverse_2_0, normed_send_0 = run_forward(
        0, core, mixed, current, w_in_t, w_out_t
    )
    mixed = mix(following_0)
    normed_got_0, active_got_0 = other_core(normed_send_0), other_core(active_0)
    normed_1, active_1, dsecond_low_1, dhidden_1, dsummed_1, halves_send_1 = run_turn(
        1, core, moved, mixed, following_0, out_grad, grad_got, w_in_t, w_out_t, w_in, w_out
    )
    returned = mix(dsummed_1)
    halves_got_1, dhidden_got_1, active_got_1 = [
        other_core(value) for value in (halves_send_1, dhidden_1, active_1)
    ]
    sums_1 = grads(core, normed_1, dhidden_1, active_1, dsecond_low_1,
                   halves_got_1, dhidden_got_1, active_got_1, halves_got_1)
    swapped_1 = [swap(value) for value in sums_1]
    returned, _ = lax.optimization_barrier((returned, sums_1))
    dsecond_low_0, dhidden_0, dsummed_0, dsecond_send_0 = run_backward(
        0, core, dsummed_1, returned, following_0, normed_0, derivative_0, inverse_s_0, inverse_2_0, w_in, w_out
    )
    dsummed_0, swapped_1[0] = lax.optimization_barrier((dsummed_0, swapped_1[0]))
    returned = mix(dsummed_0)
    dsecond_low_0, swapped_1[1] = lax.optimization_barrier((dsecond_low_0, swapped_1[1]))
    sums_0 = grads(core, normed_0, dhidden_0, active_0, dsecond_low_0,
                   normed_got_0, other_core(dhidden_0), active_got_0, other_core(dsecond_send_0))
    swapped_0 = [swap(value) for value in sums_0]
    grad_rows = (dsummed_0.astype(F32) + returned.astype(F32)).astype(BF)
    grad_rows = chosen(swap(grad_rows), grad_rows)
    grad_in = chosen(jnp.stack([swapped_0[0], swapped_1[0]]), jnp.stack([sums_0[0], sums_1[0]]))
    grad_out = chosen(jnp.stack([swapped_0[1], swapped_1[1]]), jnp.stack([sums_0[1], sums_1[1]]))
    return grad_rows[None], grad_in[:, None], grad_out[:, None]


def solution(mesh):
    return jax.shard_map(
        per_device,
        mesh=mesh,
        in_specs=(
            P("tok", None, "dp"),
            P("tok", None, "dp"),
            P(None, "tok", None, None),
            P(None, "tok", None, None),
        ),
        out_specs=(P("tok", None, "dp"), P(None, "tok", "dp", None), P(None, "tok", None, "dp")),
        check_vma=False,
    )
```
